256 devices in a mesh: gx: 16 (over x_hi, y, core), gy: 16 (over z, x_lo).
Axes of the slice: x: 4 (x_hi: 2, x_lo: 2; x = x_hi * 2 + x_lo), y: 4, z: 8, core: 2. Of those that a mesh axis runs over, the one named last changes fastest.
Arguments:
- inputs: bfloat16 [64, 64, 14, 256], P('gx', 'gy'), may hold values from -6 to 6
- cotangent: bfloat16 [64, 64, 8, 256], P('gx', 'gy'), may hold values from -6 to 6
- w_qkv: bfloat16 [256, 768], replicated, may hold values from -0.375 to 0.375
- w_out: bfloat16 [256, 256], replicated, may hold values from -0.375 to 0.375
Outputs:
- grad_inputs: bfloat16 [64, 64, 14, 256], P('gx', 'gy')
- grad_wqkv: float32 [256, 768], replicated
- grad_wout: float32 [256, 256], replicated
The draws below stay inside these ranges and needn't reach their ends.
All inputs are finite; a program needn't handle non-finite values.
Results may differ from the reference program's by a relative error of at most 0.012.
Values may be sent and summed in bfloat16 or wider, within the bound.
No kernel may reach another device: no remote copies, remote signals or barrier semaphores. Data moves between devices by JAX's collectives and lax.ppermute only.
A program may use at most 64 MiB of HBM per device.

```python
import jax
import jax.numpy as jnp
from jax import lax

C = 256
H = 4
HD = 64
RADIUS = 3
Z = 8
ZE = 14
NX = 64
NY = 64


def steps_of(stream_key, extent, cuts, low, top_value):
    def one(dim, shards_of):
        draws = jax.random.uniform(jax.random.fold_in(jax.random.fold_in(stream_key, 6), dim), (shards_of,), jnp.float32, low / len(cuts), top_value / len(cuts))
        return jnp.repeat(jnp.exp(draws), extent[dim] // shards_of).reshape((-1,) + (1,) * (len(extent) - dim - 1))

    level = one(*cuts[0])
    for cut in cuts[1:]:
        level = level * one(*cut)
    return level


def normal_values(stream_key, dims, spread, bound, cuts=(), kind=jnp.bfloat16):
    array = jax.random.normal(stream_key, dims, jnp.float32) * spread
    if len(cuts) > 0:
        array = steps_of(stream_key, dims, cuts, -0.22, 0.18) * array
    return jnp.clip(array, min=-bound, max=bound).astype(kind)


def setup_inputs(seed: int = 0) -> dict:
    seeds = jax.random.split(jax.random.key(seed), 5)
    inputs = normal_values(seeds[0], (NX, NY, ZE, C), 1.0, 6.0, ((0, 16), (1, 16)))
    cotangent = normal_values(seeds[1], (NX, NY, Z, C), 1.0, 6.0, ((0, 16), (1, 16)))
    w_qkv = normal_values(seeds[2], (C, 3 * C), C ** -0.5, 0.375)
    w_out = normal_values(seeds[3], (C, C), C ** -0.5, 0.375)
    return dict(inputs=inputs, cotangent=cotangent, w_qkv=w_qkv, w_out=w_out)


def fold_wrap(field, dim):
    count = field.shape[dim] - 2 * RADIUS
    lower_rim = lax.slice_in_dim(field, 0, RADIUS, axis=dim)
    middle = lax.slice_in_dim(field, RADIUS, RADIUS + count, axis=dim)
    upper_rim = lax.slice_in_dim(field, RADIUS + count, count + 2 * RADIUS, axis=dim)
    head_part = lax.slice_in_dim(middle, 0, RADIUS, axis=dim) + upper_rim
    middle = lax.dynamic_update_slice_in_dim(middle, head_part, 0, dim)
    tail_part = lax.slice_in_dim(middle, count - RADIUS, count, axis=dim) + lower_rim
    return lax.dynamic_update_slice_in_dim(middle, tail_part, count - RADIUS, dim)


def reference(inputs, cotangent, w_qkv, w_out):
    window_len = 2 * RADIUS + 1
    score_scale = HD ** -0.5
    hidden = jnp.dot(inputs.reshape(-1, C), w_qkv, preferred_element_type=jnp.float32).astype(jnp.bfloat16)
    hidden = hidden.reshape(NX, NY, ZE, 3 * C)
    query = hidden[:, :, RADIUS:RADIUS + Z, :C].reshape(NX, NY, Z, H, HD).astype(jnp.float32)
    padded = jnp.pad(hidden[:, :, :, C:], ((RADIUS, RADIUS), (RADIUS, RADIUS), (0, 0), (0, 0)), mode="wrap")
    grad_attn = jnp.dot(cotangent.reshape(-1, C), w_out.T, preferred_element_type=jnp.float32).astype(jnp.bfloat16)
    grad_attn = grad_attn.reshape(NX, NY, Z, H, HD).astype(jnp.float32)
    offsets = jnp.arange(window_len * window_len, dtype=jnp.int32)

    def start_of(offset):
        anchor = jnp.zeros((), jnp.int32)
        return (offset // window_len, offset % window_len, anchor, anchor)

    def block_at(offset):
        return lax.dynamic_slice(padded, start_of(offset), (NX, NY, ZE, 2 * C))

    def pieces(block, step_z):
        window = block[:, :, step_z:step_z + Z].astype(jnp.float32)
        return window[..., :C].reshape(NX, NY, Z, H, HD), window[..., C:].reshape(NX, NY, Z, H, HD)

    def score_pass(state, offset):
        block = block_at(offset)
        found = [jnp.einsum("xyzhd,xyzhd->xyzh", query, pieces(block, step_z)[0]) for step_z in range(window_len)]
        return state, jnp.stack(found) * score_scale

    scores = lax.scan(score_pass, jnp.zeros((), jnp.float32), offsets)[1]
    exps = jnp.exp(scores)
    probs = exps / jnp.sum(exps, axis=(0, 1))
    prob_bf = probs.astype(jnp.bfloat16)

    def value_pass(summed, item):
        offset, weights = item
        block = block_at(offset)
        grads = []
        for step_z in range(window_len):
            values = pieces(block, step_z)[1]
            summed = summed + weights[step_z].astype(jnp.float32)[..., None] * values
            grads.append(jnp.einsum("xyzhd,xyzhd->xyzh", grad_attn, values))
        return summed, jnp.stack(grads)

    attn_sum, grad_probs = lax.scan(value_pass, jnp.zeros((NX, NY, Z, H, HD), jnp.float32), (offsets, prob_bf))
    attended = attn_sum.astype(jnp.bfloat16).reshape(-1, C)
    grad_wout = jnp.dot(attended.T, cotangent.reshape(-1, C), preferred_element_type=jnp.float32)
    balance = jnp.sum(probs * grad_probs, axis=(0, 1))
    grad_scores = (probs * (grad_probs - balance) * score_scale).astype(jnp.bfloat16)

    def key_pass(state, item):
        grad_query, grad_padded = state
        offset, slopes, weights = item
        block = block_at(offset)
        frame = jnp.zeros((NX, NY, ZE, 2 * C), jnp.float32)
        for step_z in range(window_len):
            keys_win = pieces(block, step_z)[0]
            slope = slopes[step_z].astype(jnp.float32)[..., None]
            grad_query = grad_query + slope * keys_win
            weight = weights[step_z].astype(jnp.float32)[..., None]
            contrib = jnp.concatenate([(slope * query).reshape(NX, NY, Z, C), (weight * grad_attn).reshape(NX, NY, Z, C)], axis=-1)
            frame = frame + jnp.pad(contrib, ((0, 0), (0, 0), (step_z, ZE - Z - step_z), (0, 0)))
        start = start_of(offset)
        current = lax.dynamic_slice(grad_padded, start, frame.shape)
        grad_padded = lax.dynamic_update_slice(grad_padded, current + frame, start)
        return (grad_query, grad_padded), jnp.zeros((), jnp.float32)

    initial = (jnp.zeros((NX, NY, Z, H, HD), jnp.float32), jnp.zeros((NX + 2 * RADIUS, NY + 2 * RADIUS, ZE, 2 * C), jnp.float32))
    finals = lax.scan(key_pass, initial, (offsets, grad_scores, prob_bf))[0]
    grad_keyval = fold_wrap(fold_wrap(finals[1], 0), 1)
    grad_query = jnp.pad(finals[0].reshape(NX, NY, Z, C), ((0, 0), (0, 0), (RADIUS, RADIUS), (0, 0)))
    grad_hidden = jnp.concatenate([grad_query, grad_keyval], axis=-1).reshape(-1, 3 * C)
    grad_inputs = jnp.dot(grad_hidden, w_qkv.astype(jnp.float32).T, precision=lax.Precision.HIGHEST)
    grad_inputs = grad_inputs.astype(jnp.bfloat16).reshape(NX, NY, ZE, C)
    grad_wqkv = jnp.dot(inputs.reshape(-1, C).astype(jnp.float32).T, grad_hidden, precision=lax.Precision.HIGHEST)
    return grad_inputs, grad_wqkv, grad_wout
```

```python
import jax
import jax.numpy as jnp
from jax import lax
from jax.experimental import pallas as pl
from jax.experimental.pallas import tpu as pltpu
from jax.sharding import Mesh, PartitionSpec as P

H = 4
HD = 64
C = H * HD
RADIUS = 3
CELLS = 4
WIDE = CELLS + 2 * RADIUS
Z = 8
ZE = 14
ZP = 16
ROWS = WIDE * ZP
KEYS = WIDE * ROWS
QUERIES = CELLS * CELLS * Z
LANES = H * QUERIES
FAR = -1e30

NT = (((1,), (1,)), ((), ()))
TN = (((0,), (0,)), ((), ()))
F32 = jnp.float32
BF16 = jnp.bfloat16


def mm(a, b, dims=(((1,), (0,)), ((), ()))):
    return lax.dot_general(a, b, dims, preferred_element_type=F32)


def local_kernel(
    own, ylo, yhi, xlo, xhi, cot, wqkv, wout,
    grad_lo, grad_mid, grad_hi, dw,
    xs, ks, vs, qbd, gabd, es, gps, pbs, dss, gkvs,
):
    xs[...] = jnp.zeros_like(xs)
    xs[0:RADIUS, :, 0:ZE, :] = xlo[...]
    xs[RADIUS + CELLS :, :, 0:ZE, :] = xhi[...]
    xs[RADIUS : RADIUS + CELLS, 0:RADIUS, 0:ZE, :] = ylo[...]
    xs[RADIUS : RADIUS + CELLS, RADIUS : RADIUS + CELLS, 0:ZE, :] = own[...]
    xs[RADIUS : RADIUS + CELLS, RADIUS + CELLS :, 0:ZE, :] = yhi[...]

    inner = own[...].astype(F32)[:, :, RADIUS : RADIUS + Z, :].reshape(QUERIES, C).astype(BF16)
    cot2 = cot[...].astype(F32).reshape(QUERIES, C).astype(BF16)
    query = mm(inner, wqkv[:, :C]).astype(BF16).astype(F32) * HD ** (-0.5)
    grad_attn = mm(cot2, wout[...], NT).astype(BF16).astype(F32)
    head = lax.broadcasted_iota(jnp.int32, (QUERIES, C), 1) // HD
    for h in range(H):
        rows = slice(h * QUERIES, (h + 1) * QUERIES)
        qbd[rows, :] = jnp.where(head == h, query, 0.0).astype(BF16)
        gabd[rows, :] = jnp.where(head == h, grad_attn, 0.0).astype(BF16)

    lane = lax.broadcasted_iota(jnp.int32, (1, QUERIES), 1)
    query_x = lane // (CELLS * Z)
    query_y = lane // Z % CELLS
    query_z = lax.broadcasted_iota(jnp.int32, (ZP, QUERIES), 1) % Z

    def outside(step):
        return jnp.where((step >= 0) & (step <= 2 * RADIUS), 0.0, FAR)

    far_z = outside(lax.broadcasted_iota(jnp.int32, (ZP, QUERIES), 0) - query_z)
    far_yz = [far_z + outside(ky - query_y) for ky in range(WIDE)]

    total = jnp.zeros((8, LANES), F32)
    weighted = jnp.zeros((8, LANES), F32)
    for kx in range(WIDE):
        rows = slice(kx * ROWS, (kx + 1) * ROWS)
        kv = mm(xs[kx].reshape(ROWS, C), wqkv[:, C:]).astype(BF16)
        ks[rows, :] = kv[:, :C]
        vs[rows, :] = kv[:, C:]
        far_x = outside(kx - query_x)
        far = jnp.concatenate([part + far_x for part in far_yz], axis=0)
        scores = mm(kv[:, :C], qbd[...], NT) + jnp.concatenate([far] * H, axis=1)
        exps = jnp.exp(scores)
        grad_probs = mm(kv[:, C:], gabd[...], NT)
        es[rows, :] = exps
        gps[rows, :] = grad_probs
        total += jnp.sum(exps.reshape(ROWS // 8, 8, LANES), axis=0)
        weighted += jnp.sum((exps * grad_probs).reshape(ROWS // 8, 8, LANES), axis=0)

    inverse = 1.0 / jnp.sum(total, axis=0, keepdims=True)
    balance = jnp.sum(weighted, axis=0, keepdims=True) * inverse

    for kx in range(WIDE):
        rows = slice(kx * ROWS, (kx + 1) * ROWS)
        probs = es[rows, :] * inverse
        prob_bf = probs.astype(BF16)
        slopes = (probs * (gps[rows, :] - balance)).astype(BF16)
        pbs[rows, :] = prob_bf
        dss[rows, :] = slopes
        grad_kv = jnp.concatenate(
            [mm(slopes, qbd[...]).astype(BF16), mm(prob_bf, gabd[...]).astype(BF16)], axis=1
        )
        gkvs[rows, :] = grad_kv
        grad_in = mm(grad_kv, wqkv[:, C:], NT).reshape(WIDE, ZP, C)
        if kx < RADIUS:
            grad_lo[kx] = grad_in.astype(BF16)
        elif kx < RADIUS + CELLS:
            grad_mid[kx - RADIUS] = grad_in
        else:
            grad_hi[kx - RADIUS - CELLS] = grad_in.astype(BF16)

    def diagonal(full):
        return jnp.concatenate(
            [full[h * HD : (h + 1) * HD, h * QUERIES : (h + 1) * QUERIES] for h in range(H)], axis=0
        )

    attended = diagonal(mm(vs[...], pbs[...], TN)).astype(BF16)
    dw_out = mm(attended, cot2).astype(BF16)
    grad_query = (diagonal(mm(ks[...], dss[...], TN)) * HD ** (-0.5)).T.astype(BF16)
    grad_in_query = mm(grad_query, wqkv[:, :C], NT).reshape(CELLS, CELLS, Z, C)
    grad_mid[:, RADIUS : RADIUS + CELLS, RADIUS : RADIUS + Z, :] += grad_in_query
    dw_q = mm(inner, grad_query, TN).astype(BF16)
    dw_kv = mm(xs[...].reshape(KEYS, C), gkvs[...], TN).astype(BF16)
    parts = (dw_q, dw_kv, dw_out)
    slot = 0
    for part in parts:
        for start in range(0, part.shape[1], 128):
            dw[slot] = part[:, start : start + 128]
            slot += 1


def local_grads(own, ylo, yhi, xlo, xhi, cot, wqkv, wout):
    whole = pl.BlockSpec(memory_space=pltpu.VMEM)
    return pl.pallas_call(
        local_kernel,
        out_shape=(
            jax.ShapeDtypeStruct((RADIUS, WIDE, ZP, C), BF16),
            jax.ShapeDtypeStruct((CELLS, WIDE, ZP, C), F32),
            jax.ShapeDtypeStruct((RADIUS, WIDE, ZP, C), BF16),
            jax.ShapeDtypeStruct((8, C, 128), BF16),
        ),
        in_specs=[whole] * 8,
        out_specs=(whole,) * 4,
        scratch_shapes=[
            pltpu.VMEM((WIDE, WIDE, ZP, C), BF16),
            pltpu.VMEM((KEYS, C), BF16),
            pltpu.VMEM((KEYS, C), BF16),
            pltpu.VMEM((LANES, C), BF16),
            pltpu.VMEM((LANES, C), BF16),
            pltpu.VMEM((KEYS, LANES), F32),
            pltpu.VMEM((KEYS, LANES), F32),
            pltpu.VMEM((KEYS, LANES), BF16),
            pltpu.VMEM((KEYS, LANES), BF16),
            pltpu.VMEM((KEYS, 2 * C), BF16),
        ],
        compiler_params=pltpu.CompilerParams(vmem_limit_bytes=40 * 1024 * 1024),
    )(own, ylo, yhi, xlo, xhi, cot, wqkv, wout)


def shifted(block, axes, distance):
    size = lax.axis_size(axes)
    return lax.ppermute(block, axes, [(i, (i + distance) % size) for i in range(size)])


GX = ("xh", "y", "core")
GY = ("z", "xl")
PLANE = ("xh", "y", "xl")


def summed_weights(dw):
    core = lax.axis_index("core")
    halves = dw.reshape(2, 16, 64, 128)
    mine = lax.dynamic_index_in_dim(halves, core, 0, keepdims=False)
    other = lax.dynamic_index_in_dim(halves, 1 - core, 0, keepdims=False)
    swap = [(0, 1), (1, 0)]
    half = (mine.astype(F32) + lax.ppermute(other, "core", swap).astype(F32)).astype(BF16)
    chunks = lax.all_to_all(half, PLANE, 0, 0)
    chunk = jnp.sum(chunks.astype(F32), axis=0).astype(BF16)
    columns = lax.all_to_all(jnp.broadcast_to(chunk[None], (8, 64, 128)), "z", 0, 0)
    chunk = jnp.sum(columns.astype(F32), axis=0).astype(BF16)
    half = lax.all_to_all(jnp.broadcast_to(chunk[None], (16, 64, 128)), PLANE, 0, 0)
    other = lax.ppermute(half, "core", swap)
    low = jnp.where(core == 0, half, other).reshape(4, C, 128)
    high = jnp.where(core == 0, other, half).reshape(4, C, 128)
    whole = jnp.concatenate([low, high], axis=0).astype(F32)
    wide = whole.transpose(1, 0, 2).reshape(C, 4 * C)
    return wide[:, : 3 * C], wide[:, 3 * C :]


def body(inputs, cotangent, w_qkv, w_out):
    ylo = shifted(inputs[:, CELLS - RADIUS :], GY, 1)
    yhi = shifted(inputs[:, :RADIUS], GY, -1)
    wide = jnp.concatenate([ylo, inputs, yhi], axis=1)
    xlo = shifted(wide[CELLS - RADIUS :], GX, 1)
    xhi = shifted(wide[:RADIUS], GX, -1)
    grad_lo, grad_mid, grad_hi, dw = local_grads(
        inputs, ylo, yhi, xlo, xhi, cotangent, w_qkv, w_out
    )
    from_next = shifted(grad_lo, GX, -1).astype(F32)
    from_before = shifted(grad_hi, GX, 1).astype(F32)
    rest = ((0, 0), (0, 0), (0, 0))
    grad_mid = (
        grad_mid
        + jnp.pad(from_next, ((CELLS - RADIUS, 0),) + rest)
        + jnp.pad(from_before, ((0, CELLS - RADIUS),) + rest)
    )
    middle = grad_mid[:, RADIUS : RADIUS + CELLS]
    from_next = shifted(grad_mid[:, :RADIUS].astype(BF16), GY, -1).astype(F32)
    from_before = shifted(grad_mid[:, RADIUS + CELLS :].astype(BF16), GY, 1).astype(F32)
    rest = ((0, 0), (0, 0))
    grad_inputs = (
        middle
        + jnp.pad(from_next, ((0, 0), (CELLS - RADIUS, 0)) + rest)
        + jnp.pad(from_before, ((0, 0), (0, CELLS - RADIUS)) + rest)
    )
    grad_inputs = grad_inputs[:, :, :ZE].astype(BF16)
    grad_wqkv, grad_wout = summed_weights(dw)
    return grad_inputs, grad_wqkv, grad_wout


def solution(mesh):
    fine = Mesh(mesh.devices.reshape(2, 4, 2, 8, 2), ("xh", "y", "core", "z", "xl"))
    split = P(GX, GY, None, None)
    return jax.shard_map(
        body,
        mesh=fine,
        in_specs=(split, split, P(), P()),
        out_specs=(split, P(), P()),
        check_vma=False,
    )
```

```python
import jax
import jax.numpy as jnp
from jax import lax
from jax.experimental import pallas as pl
from jax.experimental.pallas import tpu as pltpu
from jax.sharding import Mesh, PartitionSpec as P

H = 4
HD = 64
C = H * HD
RADIUS = 3
CELLS = 4
WIDE = CELLS + 2 * RADIUS
Z = 8
ZE = 14
ZP = 16
ROWS = WIDE * ZP
KEYS = WIDE * ROWS
QUERIES = CELLS * CELLS * Z
LANES = H * QUERIES
FAR = -1e30

NT = (((1,), (1,)), ((), ()))
TN = (((0,), (0,)), ((), ()))
F32 = jnp.float32
BF16 = jnp.bfloat16


def mm(a, b, dims=(((1,), (0,)), ((), ()))):
    return lax.dot_general(a, b, dims, preferred_element_type=F32)


def local_kernel(
    own, ylo, yhi, xlo, xhi, cot, wqkv, wout,
    grad_lo, grad_mid, grad_hi, dw,
    xs, ks, vs, qbd, gabd, es, gps, pbs, dss, gkvs,
):
    xs[...] = jnp.zeros_like(xs)
    xs[0:RADIUS, :, 0:ZE, :] = xlo[...]
    xs[RADIUS + CELLS :, :, 0:ZE, :] = xhi[...]
    xs[RADIUS : RADIUS + CELLS, 0:RADIUS, 0:ZE, :] = ylo[...]
    xs[RADIUS : RADIUS + CELLS, RADIUS : RADIUS + CELLS, 0:ZE, :] = own[...]
    xs[RADIUS : RADIUS + CELLS, RADIUS + CELLS :, 0:ZE, :] = yhi[...]

    inner = own[...].astype(F32)[:, :, RADIUS : RADIUS + Z, :].reshape(QUERIES, C).astype(BF16)
    cot2 = cot[...].astype(F32).reshape(QUERIES, C).astype(BF16)
    query = mm(inner, wqkv[:, :C]).astype(BF16).astype(F32) * HD ** (-0.5)
    grad_attn = mm(cot2, wout[...], NT).astype(BF16).astype(F32)
    head = lax.broadcasted_iota(jnp.int32, (QUERIES, C), 1) // HD
    for h in range(H):
        rows = slice(h * QUERIES, (h + 1) * QUERIES)
        qbd[rows, :] = jnp.where(head == h, query, 0.0).astype(BF16)
        gabd[rows, :] = jnp.where(head == h, grad_attn, 0.0).astype(BF16)

    lane = lax.broadcasted_iota(jnp.int32, (1, QUERIES), 1)
    query_x = lane // (CELLS * Z)
    query_y = lane // Z % CELLS
    query_z = lax.broadcasted_iota(jnp.int32, (ZP, QUERIES), 1) % Z

    def outside(step):
        return jnp.where((step >= 0) & (step <= 2 * RADIUS), 0.0, FAR)

    far_z = outside(lax.broadcasted_iota(jnp.int32, (ZP, QUERIES), 0) - query_z)
    far_yz = [far_z + outside(ky - query_y) for ky in range(WIDE)]

    kv = mm(xs[...].reshape(KEYS, C), wqkv[:, C:]).astype(BF16)
    ks[...] = kv[:, :C]
    vs[...] = kv[:, C:]
    scores = mm(kv[:, :C], qbd[...], NT)
    grad_probs = mm(kv[:, C:], gabd[...], NT)
    far = jnp.concatenate([part + outside(kx - query_x) for kx in range(WIDE) for part in far_yz], axis=0)
    exps = jnp.exp(scores + jnp.concatenate([far] * H, axis=1))
    es[...] = exps
    gps[...] = grad_probs
    inverse = 1.0 / jnp.sum(exps, axis=0, keepdims=True)
    balance = jnp.sum(exps * grad_probs, axis=0, keepdims=True) * inverse

    probs = es[...] * inverse
    prob_bf = probs.astype(BF16)
    slopes = (probs * (gps[...] - balance)).astype(BF16)
    pbs[...] = prob_bf
    dss[...] = slopes
    grad_kv = jnp.concatenate(
        [mm(slopes, qbd[...]).astype(BF16), mm(prob_bf, gabd[...]).astype(BF16)], axis=1
    )
    gkvs[...] = grad_kv
    grad_in = mm(grad_kv, wqkv[:, C:], NT).reshape(WIDE, WIDE, ZP, C)
    grad_lo[...] = grad_in[:RADIUS].astype(BF16)
    grad_mid[...] = grad_in[RADIUS : RADIUS + CELLS]
    grad_hi[...] = grad_in[RADIUS + CELLS :].astype(BF16)

    def over_keys(values, weights):
        out = []
        for pair in range(H // 2):
            full = mm(
                values[:, pair * 2 * HD : (pair + 1) * 2 * HD],
                weights[:, pair * 2 * QUERIES : (pair + 1) * 2 * QUERIES],
                TN,
            )
            out += [full[:HD, :QUERIES], full[HD:, QUERIES:]]
        return jnp.concatenate(out, axis=0)

    attended = over_keys(vs, pbs).astype(BF16)
    dw_out = mm(attended, cot2).astype(BF16)
    grad_query = (over_keys(ks, dss) * HD ** (-0.5)).T.astype(BF16)
    grad_in_query = mm(grad_query, wqkv[:, :C], NT).reshape(CELLS, CELLS, Z, C)
    grad_mid[:, RADIUS : RADIUS + CELLS, RADIUS : RADIUS + Z, :] += grad_in_query
    dw_q = mm(inner, grad_query, TN).astype(BF16)
    dw_kv = mm(xs[...].reshape(KEYS, C), gkvs[...], TN).astype(BF16)
    slot = 0
    for part in (dw_q, dw_kv, dw_out):
        for start in range(0, part.shape[1], 128):
            for half in range(2):
                dw[half, slot] = part[half * 128 : (half + 1) * 128, start : start + 128]
            slot += 1


def local_grads(own, ylo, yhi, xlo, xhi, cot, wqkv, wout):
    whole = pl.BlockSpec(memory_space=pltpu.VMEM)
    return pl.pallas_call(
        local_kernel,
        out_shape=(
            jax.ShapeDtypeStruct((RADIUS, WIDE, ZP, C), BF16),
            jax.ShapeDtypeStruct((CELLS, WIDE, ZP, C), F32),
            jax.ShapeDtypeStruct((RADIUS, WIDE, ZP, C), BF16),
            jax.ShapeDtypeStruct((2, 8, 128, 128), BF16),
        ),
        in_specs=[whole] * 8,
        out_specs=(whole,) * 4,
        scratch_shapes=[
            pltpu.VMEM((WIDE, WIDE, ZP, C), BF16),
            pltpu.VMEM((KEYS, C), BF16),
            pltpu.VMEM((KEYS, C), BF16),
            pltpu.VMEM((LANES, C), BF16),
            pltpu.VMEM((LANES, C), BF16),
            pltpu.VMEM((KEYS, LANES), F32),
            pltpu.VMEM((KEYS, LANES), F32),
            pltpu.VMEM((KEYS, LANES), BF16),
            pltpu.VMEM((KEYS, LANES), BF16),
            pltpu.VMEM((KEYS, 2 * C), BF16),
        ],
        compiler_params=pltpu.CompilerParams(vmem_limit_bytes=40 * 1024 * 1024),
    )(own, ylo, yhi, xlo, xhi, cot, wqkv, wout)


def neighbours(easy, hard, axes):
    size = lax.axis_size(axes)
    near = [(i, i ^ 1) for i in range(size)]
    far = [(i, (i + 1 if i % 2 else i - 1) % size) for i in range(size)]
    from_far = lax.ppermute(hard, axes, far)
    return lax.ppermute(easy, axes, near), from_far


def exchanged(low, high, axes):
    first = lax.axis_index(axes) % 2 == 0
    near, far = neighbours(jnp.where(first, high, low), jnp.where(first, low, high), axes)
    return jnp.where(first, far, near), jnp.where(first, near, far)


def rims(block, dim, axes):
    odd = lax.axis_index(axes) % 2
    easy = lax.dynamic_slice_in_dim(block, 1 - odd, RADIUS, dim)
    hard = lax.dynamic_slice_in_dim(block, odd, RADIUS, dim)
    near, far = neighbours(easy, hard, axes)
    return jnp.where(odd == 0, far, near), jnp.where(odd == 0, near, far)


def place_kernel(half, other, wqkv, wout):
    core = lax.axis_index("core")
    for part, place in ((half, core), (other, 1 - core)):
        rows = pl.ds(pl.multiple_of(place * 128, 128), 128)
        for slot in range(8):
            tile = part[slot].astype(F32)
            if slot < 6:
                wqkv[rows, slot * 128 : (slot + 1) * 128] = tile
            else:
                wout[rows, (slot - 6) * 128 : (slot - 5) * 128] = tile


def placed(half, other):
    whole = pl.BlockSpec(memory_space=pltpu.VMEM)
    return pl.pallas_call(
        place_kernel,
        out_shape=(jax.ShapeDtypeStruct((C, 3 * C), F32), jax.ShapeDtypeStruct((C, C), F32)),
        in_specs=[whole] * 2,
        out_specs=(whole,) * 2,
        compiler_params=pltpu.CompilerParams(vmem_limit_bytes=8 * 1024 * 1024),
    )(half.reshape(8, 128, 128), other.reshape(8, 128, 128))


GX = ("xh", "y", "core")
GY = ("z", "xl")
PLANE = ("xh", "y", "xl")


def summed_weights(dw):
    core = lax.axis_index("core")
    halves = dw.reshape(2, 16, 64, 128)
    mine = lax.dynamic_index_in_dim(halves, core, 0, keepdims=False)
    other = lax.dynamic_index_in_dim(halves, 1 - core, 0, keepdims=False)
    swap = [(0, 1), (1, 0)]
    half = (mine.astype(F32) + lax.ppermute(other, "core", swap).astype(F32)).astype(BF16)
    chunks = lax.all_to_all(half, PLANE, 0, 0)
    chunk = jnp.sum(chunks.astype(F32), axis=0).astype(BF16)
    columns = lax.all_to_all(jnp.broadcast_to(chunk[None], (8, 64, 128)), "z", 0, 0)
    chunk = jnp.sum(columns.astype(F32), axis=0).astype(BF16)
    half = lax.all_to_all(jnp.broadcast_to(chunk[None], (16, 64, 128)), PLANE, 0, 0)
    other = lax.ppermute(half, "core", swap)
    return placed(half, other)


def body(inputs, cotangent, w_qkv, w_out):
    ylo, yhi = rims(inputs, 1, GY)
    wide = jnp.concatenate([ylo, inputs, yhi], axis=1)
    xlo, xhi = rims(wide, 0, GX)
    grad_lo, grad_mid, grad_hi, dw = local_grads(
        inputs, ylo, yhi, xlo, xhi, cotangent, w_qkv, w_out
    )
    from_before, from_next = exchanged(grad_lo, grad_hi, GX)
    from_before, from_next = from_before.astype(F32), from_next.astype(F32)
    rest = ((0, 0), (0, 0), (0, 0))
    grad_mid = (
        grad_mid
        + jnp.pad(from_next, ((CELLS - RADIUS, 0),) + rest)
        + jnp.pad(from_before, ((0, CELLS - RADIUS),) + rest)
    )
    middle = grad_mid[:, RADIUS : RADIUS + CELLS]
    low = grad_mid[:, :RADIUS].astype(BF16)
    high = grad_mid[:, RADIUS + CELLS :].astype(BF16)
    from_before, from_next = exchanged(low, high, GY)
    from_before, from_next = from_before.astype(F32), from_next.astype(F32)
    rest = ((0, 0), (0, 0))
    grad_inputs = (
        middle
        + jnp.pad(from_next, ((0, 0), (CELLS - RADIUS, 0)) + rest)
        + jnp.pad(from_before, ((0, 0), (0, CELLS - RADIUS)) + rest)
    )
    grad_inputs = grad_inputs[:, :, :ZE].astype(BF16)
    grad_wqkv, grad_wout = summed_weights(dw)
    return grad_inputs, grad_wqkv, grad_wout


def solution(mesh):
    fine = Mesh(mesh.devices.reshape(2, 4, 2, 8, 2), ("xh", "y", "core", "z", "xl"))
    split = P(GX, GY, None, None)
    return jax.shard_map(
        body,
        mesh=fine,
        in_specs=(split, split, P(), P()),
        out_specs=(split, P(), P()),
        check_vma=False,
    )
```

```python
import jax
import jax.numpy as jnp
from jax import lax
from jax.experimental import pallas as pl
from jax.experimental.pallas import tpu as pltpu
from jax.sharding import Mesh, PartitionSpec as P

H = 4
HD = 64
C = H * HD
RADIUS = 3
CELLS = 4
WIDE = CELLS + 2 * RADIUS
Z = 8
ZE = 14
ZP = 16
ROWS = WIDE * ZP
KEYS = WIDE * ROWS
QUERIES = CELLS * CELLS * Z
LANES = H * QUERIES
FAR = -1e30

NT = (((1,), (1,)), ((), ()))
TN = (((0,), (0,)), ((), ()))
F32 = jnp.float32
BF16 = jnp.bfloat16


def mm(a, b, dims=(((1,), (0,)), ((), ()))):
    return lax.dot_general(a, b, dims, preferred_element_type=F32)


def far_along(step):
    return jnp.where((step >= 0) & (step <= 2 * RADIUS), 0.0, FAR)


def outside(rows_x):
    lane = lax.broadcasted_iota(jnp.int32, (1, QUERIES), 1)
    query_z = lax.broadcasted_iota(jnp.int32, (ZP, QUERIES), 1) % Z
    far_z = far_along(lax.broadcasted_iota(jnp.int32, (ZP, QUERIES), 0) - query_z)
    far_yz = [far_z + far_along(ky - lane // Z % CELLS) for ky in range(WIDE)]
    far_x = [far_along(kx - lane // (CELLS * Z)) for kx in rows_x]
    far = jnp.concatenate([yz + x for x in far_x for yz in far_yz], axis=0)
    return jnp.concatenate([far] * H, axis=1)


def forward(inputs, rows_x, w_kv, qbd, gabd, ks, vs, es, gps):
    kv = mm(inputs, w_kv).astype(BF16)
    ks[...] = kv[:, :C]
    vs[...] = kv[:, C:]
    scores = mm(kv[:, :C], qbd, NT)
    grad_probs = mm(kv[:, C:], gabd, NT)
    exps = jnp.exp(scores + outside(rows_x))
    es[...] = exps
    gps[...] = grad_probs
    weighted = jnp.sum(exps * grad_probs, axis=0, keepdims=True)
    return jnp.sum(exps, axis=0, keepdims=True), weighted


CENTRE = range(RADIUS, RADIUS + CELLS)
OUTER = [*range(RADIUS), *range(RADIUS + CELLS, WIDE)]


def centre_kernel(own, ylo, yhi, cot, wqkv, wout, xs, qbd, gabd, ks, vs, es, gps, sums):
    xs[...] = jnp.zeros_like(xs)
    xs[:, 0:RADIUS, 0:ZE, :] = ylo[...]
    xs[:, RADIUS : RADIUS + CELLS, 0:ZE, :] = own[...]
    xs[:, RADIUS + CELLS :, 0:ZE, :] = yhi[...]
    inner = own[...].astype(F32)[:, :, RADIUS : RADIUS + Z, :].reshape(QUERIES, C).astype(BF16)
    cot2 = cot[...].astype(F32).reshape(QUERIES, C).astype(BF16)
    query = mm(inner, wqkv[:, :C]).astype(BF16).astype(F32) * HD ** (-0.5)
    grad_attn = mm(cot2, wout[...], NT).astype(BF16).astype(F32)
    head = lax.broadcasted_iota(jnp.int32, (QUERIES, C), 1) // HD
    for h in range(H):
        rows = slice(h * QUERIES, (h + 1) * QUERIES)
        qbd[rows, :] = jnp.where(head == h, query, 0.0).astype(BF16)
        gabd[rows, :] = jnp.where(head == h, grad_attn, 0.0).astype(BF16)
    exp_sum, weighted = forward(
        xs[...].reshape(-1, C), CENTRE, wqkv[:, C:], qbd[...], gabd[...], ks, vs, es, gps
    )
    sums[0:1, :] = exp_sum
    sums[1:2, :] = weighted


def main_kernel(
    own, cot, wqkv, xlo, xhi, xc, qbd, gabd, kc, vc, ec, gpc, sums,
    gkvc, gkvo, grad_query, dw,
    xo, ko, vo, eo, gpo, pbc, pbo, dsc, dso,
):
    xo[...] = jnp.zeros_like(xo)
    xo[0:RADIUS, :, 0:ZE, :] = xlo[...]
    xo[RADIUS:, :, 0:ZE, :] = xhi[...]
    exp_sum, weighted = forward(
        xo[...].reshape(-1, C), OUTER, wqkv[:, C:], qbd[...], gabd[...], ko, vo, eo, gpo
    )
    inverse = 1.0 / (sums[0:1, :] + exp_sum)
    balance = (sums[1:2, :] + weighted) * inverse
    for es, gps, pbs, dss, gkvs in ((ec, gpc, pbc, dsc, gkvc), (eo, gpo, pbo, dso, gkvo)):
        probs = es[...] * inverse
        prob_bf = probs.astype(BF16)
        slopes = (probs * (gps[...] - balance)).astype(BF16)
        pbs[...] = prob_bf
        dss[...] = slopes
        gkvs[:, :C] = mm(slopes, qbd[...]).astype(BF16)
        gkvs[:, C:] = mm(prob_bf, gabd[...]).astype(BF16)

    def over_keys(parts):
        out = []
        for pair in range(H // 2):
            channels = slice(pair * 2 * HD, (pair + 1) * 2 * HD)
            lanes = slice(pair * 2 * QUERIES, (pair + 1) * 2 * QUERIES)
            full = sum(mm(values[:, channels], weights[:, lanes], TN) for values, weights in parts)
            out += [full[:HD, :QUERIES], full[HD:, QUERIES:]]
        return jnp.concatenate(out, axis=0)

    inner = own[...].astype(F32)[:, :, RADIUS : RADIUS + Z, :].reshape(QUERIES, C).astype(BF16)
    cot2 = cot[...].astype(F32).reshape(QUERIES, C).astype(BF16)
    attended = over_keys(((vc, pbc), (vo, pbo))).astype(BF16)
    dw_out = mm(attended, cot2).astype(BF16)
    grad_q = (over_keys(((kc, dsc), (ko, dso))) * HD ** (-0.5)).T.astype(BF16)
    grad_query[...] = grad_q
    dw_q = mm(inner, grad_q, TN).astype(BF16)
    dw_kv = mm(xc[...].reshape(-1, C), gkvc[...], TN) + mm(xo[...].reshape(-1, C), gkvo[...], TN)
    slot = 0
    for part in (dw_q, dw_kv.astype(BF16), dw_out):
        for start in range(0, part.shape[1], 128):
            for half in range(2):
                dw[half, slot] = part[half * 128 : (half + 1) * 128, start : start + 128]
            slot += 1


def inputs_kernel(gkvc, gkvo, grad_query, wqkv, grad_lo, grad_mid, grad_hi):
    outer = mm(gkvo[...], wqkv[:, C:], NT).astype(BF16).reshape(2 * RADIUS, WIDE, ZP, C)
    grad_lo[...] = outer[:RADIUS]
    grad_hi[...] = outer[RADIUS:]
    grad_mid[...] = mm(gkvc[...], wqkv[:, C:], NT).reshape(CELLS, WIDE, ZP, C)
    from_query = mm(grad_query[...], wqkv[:, :C], NT).reshape(CELLS, CELLS, Z, C)
    grad_mid[:, RADIUS : RADIUS + CELLS, RADIUS : RADIUS + Z, :] += from_query


def kernel_call(kernel, outs, args, scratch=(), flops=0, mib=24):
    whole = pl.BlockSpec(memory_space=pltpu.VMEM)
    return pl.pallas_call(
        kernel,
        out_shape=tuple(jax.ShapeDtypeStruct(shape, kind) for shape, kind in outs),
        in_specs=[whole] * len(args),
        out_specs=(whole,) * len(outs),
        scratch_shapes=[pltpu.VMEM(shape, kind) for shape, kind in scratch],
        cost_estimate=pl.CostEstimate(flops=flops, bytes_accessed=4 * 2**20, transcendentals=0),
        compiler_params=pltpu.CompilerParams(vmem_limit_bytes=mib * 2**20),
    )(*args)


NC_ = CELLS * ROWS
NO_ = 2 * RADIUS * ROWS


def centre(own, ylo, yhi, cot, wqkv, wout):
    outs = (
        ((CELLS, WIDE, ZP, C), BF16),
        ((LANES, C), BF16),
        ((LANES, C), BF16),
        ((NC_, C), BF16),
        ((NC_, C), BF16),
        ((NC_, LANES), F32),
        ((NC_, LANES), F32),
        ((2, LANES), F32),
    )
    return kernel_call(centre_kernel, outs, (own, ylo, yhi, cot, wqkv, wout), flops=10**9)


def main(own, cot, wqkv, xlo, xhi, held):
    outs = (
        ((NC_, 2 * C), BF16),
        ((NO_, 2 * C), BF16),
        ((QUERIES, C), BF16),
        ((2, 8, 128, 128), BF16),
    )
    scratch = (
        ((2 * RADIUS, WIDE, ZP, C), BF16),
        ((NO_, C), BF16),
        ((NO_, C), BF16),
        ((NO_, LANES), F32),
        ((NO_, LANES), F32),
        ((NC_, LANES), BF16),
        ((NO_, LANES), BF16),
        ((NC_, LANES), BF16),
        ((NO_, LANES), BF16),
    )
    args = (own, cot, wqkv, xlo, xhi, *held)
    return kernel_call(main_kernel, outs, args, scratch, flops=3 * 10**9)


def through_inputs(gkvc, gkvo, grad_query, wqkv):
    outs = (
        ((RADIUS, WIDE, ZP, C), BF16),
        ((CELLS, WIDE, ZP, C), F32),
        ((RADIUS, WIDE, ZP, C), BF16),
    )
    return kernel_call(inputs_kernel, outs, (gkvc, gkvo, grad_query, wqkv), flops=10**9)


def local_grads(own, ylo, yhi, xlo, xhi, cot, wqkv, wout):
    held = centre(own, ylo, yhi, cot, wqkv, wout)
    gkvc, gkvo, grad_query, dw = main(own, cot, wqkv, xlo, xhi, held)
    return (*through_inputs(gkvc, gkvo, grad_query, wqkv), dw)


def neighbours(easy, hard, axes):
    size = lax.axis_size(axes)
    near = [(i, i ^ 1) for i in range(size)]
    far = [(i, (i + 1 if i % 2 else i - 1) % size) for i in range(size)]
    from_far = lax.ppermute(hard, axes, far)
    return lax.ppermute(easy, axes, near), from_far


def exchanged(low, high, axes):
    first = lax.axis_index(axes) % 2 == 0
    near, far = neighbours(jnp.where(first, high, low), jnp.where(first, low, high), axes)
    return jnp.where(first, far, near), jnp.where(first, near, far)


def rims(block, dim, axes):
    odd = lax.axis_index(axes) % 2
    easy = lax.dynamic_slice_in_dim(block, 1 - odd, RADIUS, dim)
    hard = lax.dynamic_slice_in_dim(block, odd, RADIUS, dim)
    near, far = neighbours(easy, hard, axes)
    return jnp.where(odd == 0, far, near), jnp.where(odd == 0, near, far)


def place_kernel(half, other, wqkv, wout):
    core = lax.axis_index("core")
    for part, place in ((half, core), (other, 1 - core)):
        rows = pl.ds(pl.multiple_of(place * 128, 128), 128)
        for slot in range(8):
            tile = part[slot].astype(F32)
            if slot < 6:
                wqkv[rows, slot * 128 : (slot + 1) * 128] = tile
            else:
                wout[rows, (slot - 6) * 128 : (slot - 5) * 128] = tile


def placed(half, other):
    whole = pl.BlockSpec(memory_space=pltpu.VMEM)
    return pl.pallas_call(
        place_kernel,
        out_shape=(jax.ShapeDtypeStruct((C, 3 * C), F32), jax.ShapeDtypeStruct((C, C), F32)),
        in_specs=[whole] * 2,
        out_specs=(whole,) * 2,
        compiler_params=pltpu.CompilerParams(vmem_limit_bytes=8 * 1024 * 1024),
    )(half.reshape(8, 128, 128), other.reshape(8, 128, 128))


GX = ("xh", "y", "core")
GY = ("z", "xl")
PLANE = ("xh", "y", "xl")


def summed_weights(dw):
    core = lax.axis_index("core")
    halves = dw.reshape(2, 16, 64, 128)
    mine = lax.dynamic_index_in_dim(halves, core, 0, keepdims=False)
    other = lax.dynamic_index_in_dim(halves, 1 - core, 0, keepdims=False)
    swap = [(0, 1), (1, 0)]
    half = (mine.astype(F32) + lax.ppermute(other, "core", swap).astype(F32)).astype(BF16)
    chunks = lax.all_to_all(half, PLANE, 0, 0)
    chunk = jnp.sum(chunks.astype(F32), axis=0).astype(BF16)
    columns = lax.all_to_all(jnp.broadcast_to(chunk[None], (8, 64, 128)), "z", 0, 0)
    chunk = jnp.sum(columns.astype(F32), axis=0).astype(BF16)
    half = lax.all_to_all(jnp.broadcast_to(chunk[None], (16, 64, 128)), PLANE, 0, 0)
    other = lax.ppermute(half, "core", swap)
    return placed(half, other)


def body(inputs, cotangent, w_qkv, w_out):
    ylo, yhi = rims(inputs, 1, GY)
    wide = jnp.concatenate([ylo, inputs, yhi], axis=1)
    xlo, xhi = rims(wide, 0, GX)
    grad_lo, grad_mid, grad_hi, dw = local_grads(
        inputs, ylo, yhi, xlo, xhi, cotangent, w_qkv, w_out
    )
    from_before, from_next = exchanged(grad_lo, grad_hi, GX)
    from_before, from_next = from_before.astype(F32), from_next.astype(F32)
    rest = ((0, 0), (0, 0), (0, 0))
    grad_mid = (
        grad_mid
        + jnp.pad(from_next, ((CELLS - RADIUS, 0),) + rest)
        + jnp.pad(from_before, ((0, CELLS - RADIUS),) + rest)
    )
    middle = grad_mid[:, RADIUS : RADIUS + CELLS]
    low = grad_mid[:, :RADIUS].astype(BF16)
    high = grad_mid[:, RADIUS + CELLS :].astype(BF16)
    from_before, from_next = exchanged(low, high, GY)
    from_before, from_next = from_before.astype(F32), from_next.astype(F32)
    rest = ((0, 0), (0, 0))
    grad_inputs = (
        middle
        + jnp.pad(from_next, ((0, 0), (CELLS - RADIUS, 0)) + rest)
        + jnp.pad(from_before, ((0, 0), (0, CELLS - RADIUS)) + rest)
    )
    grad_inputs = grad_inputs[:, :, :ZE].astype(BF16)
    grad_wqkv, grad_wout = summed_weights(dw)
    return grad_inputs, grad_wqkv, grad_wout


def solution(mesh):
    fine = Mesh(mesh.devices.reshape(2, 4, 2, 8, 2), ("xh", "y", "core", "z", "xl"))
    split = P(GX, GY, None, None)
    return jax.shard_map(
        body,
        mesh=fine,
        in_specs=(split, split, P(), P()),
        out_specs=(split, P(), P()),
        check_vma=False,
    )
```

```python
import jax
import jax.numpy as jnp
from jax import lax
from jax.experimental import pallas as pl
from jax.experimental.pallas import tpu as pltpu
from jax.sharding import Mesh, PartitionSpec as P

H = 4
HD = 64
C = H * HD
RADIUS = 3
CELLS = 4
WIDE = CELLS + 2 * RADIUS
Z = 8
ZE = 14
ZP = 16
ROWS = WIDE * ZP
KEYS = WIDE * ROWS
QUERIES = CELLS * CELLS * Z
LANES = H * QUERIES
FAR = -1e30

NT = (((1,), (1,)), ((), ()))
TN = (((0,), (0,)), ((), ()))
F32 = jnp.float32
BF16 = jnp.bfloat16


def mm(a, b, dims=(((1,), (0,)), ((), ()))):
    return lax.dot_general(a, b, dims, preferred_element_type=F32)


def far_along(step):
    return jnp.where((step >= 0) & (step <= 2 * RADIUS), 0.0, FAR)


def outside(rows_x):
    lane = lax.broadcasted_iota(jnp.int32, (1, QUERIES), 1)
    query_z = lax.broadcasted_iota(jnp.int32, (ZP, QUERIES), 1) % Z
    far_z = far_along(lax.broadcasted_iota(jnp.int32, (ZP, QUERIES), 0) - query_z)
    far_yz = [far_z + far_along(ky - lane // Z % CELLS) for ky in range(WIDE)]
    far_x = [far_along(kx - lane // (CELLS * Z)) for kx in rows_x]
    far = jnp.concatenate([yz + x for x in far_x for yz in far_yz], axis=0)
    return jnp.concatenate([far] * H, axis=1)


def forward(inputs, rows_x, w_kv, qbd, gabd, ks, vs, es, gps):
    kv = mm(inputs, w_kv).astype(BF16)
    ks[...] = kv[:, :C]
    vs[...] = kv[:, C:]
    scores = mm(kv[:, :C], qbd, NT)
    grad_probs = mm(kv[:, C:], gabd, NT)
    exps = jnp.exp(scores + outside(rows_x))
    es[...] = exps
    gps[...] = grad_probs
    weighted = jnp.sum(exps * grad_probs, axis=0, keepdims=True)
    return jnp.sum(exps, axis=0, keepdims=True), weighted


CENTRE = range(RADIUS, RADIUS + CELLS)
OUTER = [*range(RADIUS), *range(RADIUS + CELLS, WIDE)]


def rims_kernel(inputs, own, near, far):
    for x in range(CELLS):
        block = jnp.swapaxes(inputs[x].astype(F32), 0, 1)
        filled = jnp.concatenate([block, jnp.zeros((CELLS, ZP - ZE, C), F32)], axis=1)
        own[x] = filled.astype(BF16)
    odd = lax.axis_index("xl")
    near[...] = own[:, pl.ds(1 - odd, RADIUS)]
    far[...] = own[:, pl.ds(odd, RADIUS)]


def centre_kernel(own, ylo, yhi, cot, wqkv, wout, xs, qbd, gabd, ks, vs, es, gps, sums):
    xs[:, 0:RADIUS] = ylo[...]
    xs[:, RADIUS : RADIUS + CELLS] = own[...]
    xs[:, RADIUS + CELLS :] = yhi[...]
    inner = own[...].astype(F32)[:, :, RADIUS : RADIUS + Z, :].reshape(QUERIES, C).astype(BF16)
    cot2 = cot[...].astype(F32).reshape(QUERIES, C).astype(BF16)
    query = mm(inner, wqkv[:, :C]).astype(BF16).astype(F32) * HD ** (-0.5)
    grad_attn = mm(cot2, wout[...], NT).astype(BF16).astype(F32)
    head = lax.broadcasted_iota(jnp.int32, (QUERIES, C), 1) // HD
    for h in range(H):
        rows = slice(h * QUERIES, (h + 1) * QUERIES)
        qbd[rows, :] = jnp.where(head == h, query, 0.0).astype(BF16)
        gabd[rows, :] = jnp.where(head == h, grad_attn, 0.0).astype(BF16)
    exp_sum, weighted = forward(
        xs[...].reshape(-1, C), CENTRE, wqkv[:, C:], qbd[...], gabd[...], ks, vs, es, gps
    )
    sums[0:1, :] = exp_sum
    sums[1:2, :] = weighted


def main_kernel(
    own, cot, wqkv, xlo, xhi, xc, qbd, gabd, kc, vc, ec, gpc, sums,
    gkvc, gkvo, grad_query, dw,
    xo, ko, vo, eo, gpo, pbc, pbo, dsc, dso,
):
    xo[0:RADIUS] = xlo[...]
    xo[RADIUS:] = xhi[...]
    exp_sum, weighted = forward(
        xo[...].reshape(-1, C), OUTER, wqkv[:, C:], qbd[...], gabd[...], ko, vo, eo, gpo
    )
    inverse = 1.0 / (sums[0:1, :] + exp_sum)
    balance = (sums[1:2, :] + weighted) * inverse
    for es, gps, pbs, dss, gkvs in ((ec, gpc, pbc, dsc, gkvc), (eo, gpo, pbo, dso, gkvo)):
        probs = es[...] * inverse
        prob_bf = probs.astype(BF16)
        slopes = (probs * (gps[...] - balance)).astype(BF16)
        pbs[...] = prob_bf
        dss[...] = slopes
        gkvs[:, :C] = mm(slopes, qbd[...]).astype(BF16)
        gkvs[:, C:] = mm(prob_bf, gabd[...]).astype(BF16)

    def over_keys(parts):
        out = []
        for pair in range(H // 2):
            channels = slice(pair * 2 * HD, (pair + 1) * 2 * HD)
            lanes = slice(pair * 2 * QUERIES, (pair + 1) * 2 * QUERIES)
            full = sum(mm(values[:, channels], weights[:, lanes], TN) for values, weights in parts)
            out += [full[:HD, :QUERIES], full[HD:, QUERIES:]]
        return jnp.concatenate(out, axis=0)

    inner = own[...].astype(F32)[:, :, RADIUS : RADIUS + Z, :].reshape(QUERIES, C).astype(BF16)
    cot2 = cot[...].astype(F32).reshape(QUERIES, C).astype(BF16)
    attended = over_keys(((vc, pbc), (vo, pbo))).astype(BF16)
    grad_q = over_keys(((kc, dsc), (ko, dso))) * HD ** (-0.5)
    dw_kv = mm(xc[...].reshape(-1, C), gkvc[...], TN) + mm(xo[...].reshape(-1, C), gkvo[...], TN)
    grad_q = grad_q.T.astype(BF16)
    grad_query[...] = grad_q
    dw_out = mm(attended, cot2).astype(BF16)
    dw_q = mm(inner, grad_q, TN).astype(BF16)
    slot = 0
    for part in (dw_q, dw_kv.astype(BF16), dw_out):
        for start in range(0, part.shape[1], 128):
            for half in range(2):
                dw[half, slot] = part[half * 128 : (half + 1) * 128, start : start + 128]
            slot += 1


def inputs_kernel(gkvc, gkvo, grad_query, wqkv, grad_lo, grad_mid, grad_hi):
    outer = mm(gkvo[...], wqkv[:, C:], NT).astype(BF16).reshape(2 * RADIUS, WIDE, ZP, C)
    grad_lo[...] = outer[:RADIUS]
    grad_hi[...] = outer[RADIUS:]
    grad_mid[...] = mm(gkvc[...], wqkv[:, C:], NT).reshape(CELLS, WIDE, ZP, C)
    from_query = mm(grad_query[...], wqkv[:, :C], NT).reshape(CELLS, CELLS, Z, C)
    grad_mid[:, RADIUS : RADIUS + CELLS, RADIUS : RADIUS + Z, :] += from_query


def kernel_call(kernel, outs, args, scratch=(), flops=0, mib=24):
    whole = pl.BlockSpec(memory_space=pltpu.VMEM)
    return pl.pallas_call(
        kernel,
        out_shape=tuple(jax.ShapeDtypeStruct(shape, kind) for shape, kind in outs),
        in_specs=[whole] * len(args),
        out_specs=(whole,) * len(outs),
        scratch_shapes=[pltpu.VMEM(shape, kind) for shape, kind in scratch],
        cost_estimate=pl.CostEstimate(flops=flops, bytes_accessed=4 * 2**20, transcendentals=0),
        compiler_params=pltpu.CompilerParams(vmem_limit_bytes=mib * 2**20),
    )(*args)


NC_ = CELLS * ROWS
NO_ = 2 * RADIUS * ROWS


def centre(own, ylo, yhi, cot, wqkv, wout):
    outs = (
        ((CELLS, WIDE, ZP, C), BF16),
        ((LANES, C), BF16),
        ((LANES, C), BF16),
        ((NC_, C), BF16),
        ((NC_, C), BF16),
        ((NC_, LANES), F32),
        ((NC_, LANES), F32),
        ((2, LANES), F32),
    )
    return kernel_call(centre_kernel, outs, (own, ylo, yhi, cot, wqkv, wout), flops=10**9)


def main(own, cot, wqkv, xlo, xhi, held):
    outs = (
        ((NC_, 2 * C), BF16),
        ((NO_, 2 * C), BF16),
        ((QUERIES, C), BF16),
        ((2, 8, 128, 128), BF16),
    )
    scratch = (
        ((2 * RADIUS, WIDE, ZP, C), BF16),
        ((NO_, C), BF16),
        ((NO_, C), BF16),
        ((NO_, LANES), F32),
        ((NO_, LANES), F32),
        ((NC_, LANES), BF16),
        ((NO_, LANES), BF16),
        ((NC_, LANES), BF16),
        ((NO_, LANES), BF16),
    )
    args = (own, cot, wqkv, xlo, xhi, *held)
    return kernel_call(main_kernel, outs, args, scratch, flops=3 * 10**9)


def through_inputs(gkvc, gkvo, grad_query, wqkv):
    outs = (
        ((RADIUS, WIDE, ZP, C), BF16),
        ((CELLS, WIDE, ZP, C), F32),
        ((RADIUS, WIDE, ZP, C), BF16),
    )
    return kernel_call(inputs_kernel, outs, (gkvc, gkvo, grad_query, wqkv), flops=10**9)


def own_rims(inputs):
    rim = ((CELLS, RADIUS, ZP, C), BF16)
    outs = (((CELLS, CELLS, ZP, C), BF16), rim, rim)
    return kernel_call(rims_kernel, outs, (inputs.transpose(0, 2, 1, 3),), mib=4)


def local_grads(own, ylo, yhi, xlo, xhi, cot, wqkv, wout):
    held = centre(own, ylo, yhi, cot, wqkv, wout)
    gkvc, gkvo, grad_query, dw = main(own, cot, wqkv, xlo, xhi, held)
    return (*through_inputs(gkvc, gkvo, grad_query, wqkv), dw)


def to_near(block, axes):
    return lax.ppermute(block, axes, [(i, i ^ 1) for i in range(lax.axis_size(axes))])


def to_far(block, axes):
    size = lax.axis_size(axes)
    pairs = [(i, (i + 1 if i % 2 else i - 1) % size) for i in range(size)]
    return lax.ppermute(block, axes, pairs)


def neighbours(easy, hard, axes):
    from_far = to_far(hard, axes)
    return to_near(easy, axes), from_far


def exchanged(low, high, axes):
    first = lax.axis_index(axes) % 2 == 0
    near, far = neighbours(jnp.where(first, high, low), jnp.where(first, low, high), axes)
    return jnp.where(first, far, near), jnp.where(first, near, far)


def rims(block, dim, axes):
    odd = lax.axis_index(axes) % 2
    easy = lax.dynamic_slice_in_dim(block, 1 - odd, RADIUS, dim)
    hard = lax.dynamic_slice_in_dim(block, odd, RADIUS, dim)
    near, far = neighbours(easy, hard, axes)
    return jnp.where(odd == 0, far, near), jnp.where(odd == 0, near, far)


def last_kernel(half, other, middle, before, after, wqkv, wout, grads):
    core = lax.axis_index("core")
    for part, place in ((half, core), (other, 1 - core)):
        rows = pl.ds(pl.multiple_of(place * 128, 128), 128)
        for slot in range(8):
            tile = part[slot].astype(F32)
            if slot < 6:
                wqkv[rows, slot * 128 : (slot + 1) * 128] = tile
            else:
                wout[rows, (slot - 6) * 128 : (slot - 5) * 128] = tile
    columns = []
    for y in range(CELLS):
        column = middle[:, y]
        if y < RADIUS:
            column += before[:, y].astype(F32)
        if y >= CELLS - RADIUS:
            column += after[:, y - CELLS + RADIUS].astype(F32)
        columns.append(column[:, :ZE])
    grads[...] = jnp.stack(columns, axis=2).astype(BF16)


def last(half, other, middle, before, after):
    whole = pl.BlockSpec(memory_space=pltpu.VMEM)
    wqkv, wout, grads = pl.pallas_call(
        last_kernel,
        out_shape=(
            jax.ShapeDtypeStruct((C, 3 * C), F32),
            jax.ShapeDtypeStruct((C, C), F32),
            jax.ShapeDtypeStruct((CELLS, ZE, CELLS, C), BF16),
        ),
        in_specs=[whole] * 5,
        out_specs=(whole,) * 3,
        compiler_params=pltpu.CompilerParams(vmem_limit_bytes=10 * 2**20),
    )(half.reshape(8, 128, 128), other.reshape(8, 128, 128), middle, before, after)
    return grads.transpose(0, 2, 1, 3), wqkv, wout


GX = ("xh", "y", "core")
GY = ("z", "xl")
PLANE = ("xh", "y", "xl")


def summed_weights(dw):
    core = lax.axis_index("core")
    halves = dw.reshape(2, 16, 64, 128)
    mine = lax.dynamic_index_in_dim(halves, core, 0, keepdims=False)
    other = lax.dynamic_index_in_dim(halves, 1 - core, 0, keepdims=False)
    swap = [(0, 1), (1, 0)]
    half = (mine.astype(F32) + lax.ppermute(other, "core", swap).astype(F32)).astype(BF16)
    chunks = lax.all_to_all(half, PLANE, 0, 0)
    chunk = jnp.sum(chunks.astype(F32), axis=0).astype(BF16)
    columns = lax.all_to_all(jnp.broadcast_to(chunk[None], (8, 64, 128)), "z", 0, 0)
    chunk = jnp.sum(columns.astype(F32), axis=0).astype(BF16)
    half = lax.all_to_all(jnp.broadcast_to(chunk[None], (16, 64, 128)), PLANE, 0, 0)
    other = lax.ppermute(half, "core", swap)
    return half, other


def body(inputs, cotangent, w_qkv, w_out):
    own, near, far = own_rims(inputs)
    far, near = to_far(far, GY), to_near(near, GY)
    first = lax.axis_index(GY) % 2 == 0
    ylo, yhi = jnp.where(first, far, near), jnp.where(first, near, far)
    wide = jnp.concatenate([ylo, own, yhi], axis=1)
    xlo, xhi = rims(wide, 0, GX)
    grad_lo, grad_mid, grad_hi, dw = local_grads(
        own, ylo, yhi, xlo, xhi, cotangent, w_qkv, w_out
    )
    from_before, from_next = exchanged(grad_lo, grad_hi, GX)
    from_before, from_next = from_before.astype(F32), from_next.astype(F32)
    rest = ((0, 0), (0, 0), (0, 0))
    grad_mid = (
        grad_mid
        + jnp.pad(from_next, ((CELLS - RADIUS, 0),) + rest)
        + jnp.pad(from_before, ((0, CELLS - RADIUS),) + rest)
    )
    middle = grad_mid[:, RADIUS : RADIUS + CELLS]
    low = grad_mid[:, :RADIUS].astype(BF16)
    high = grad_mid[:, RADIUS + CELLS :].astype(BF16)
    from_before, from_next = exchanged(low, high, GY)
    half, other = summed_weights(dw)
    return last(half, other, middle, from_before, from_next)


def solution(mesh):
    fine = Mesh(mesh.devices.reshape(2, 4, 2, 8, 2), ("xh", "y", "core", "z", "xl"))
    split = P(GX, GY, None, None)
    return jax.shard_map(
        body,
        mesh=fine,
        in_specs=(split, split, P(), P()),
        out_specs=(split, P(), P()),
        check_vma=False,
    )
```

```python
import jax
import jax.numpy as jnp
from jax import lax
from jax.experimental import pallas as pl
from jax.experimental.pallas import tpu as pltpu
from jax.sharding import Mesh, PartitionSpec as P

H = 4
HD = 64
C = H * HD
RADIUS = 3
CELLS = 4
WIDE = CELLS + 2 * RADIUS
Z = 8
ZE = 14
ZP = 16
ROWS = WIDE * ZP
KEYS = WIDE * ROWS
QUERIES = CELLS * CELLS * Z
LANES = H * QUERIES
FAR = -1e30

NT = (((1,), (1,)), ((), ()))
TN = (((0,), (0,)), ((), ()))
F32 = jnp.float32
BF16 = jnp.bfloat16


def mm(a, b, dims=(((1,), (0,)), ((), ()))):
    return lax.dot_general(a, b, dims, preferred_element_type=F32)


def far_along(step):
    return jnp.where((step >= 0) & (step <= 2 * RADIUS), 0.0, FAR)


def outside(rows_x):
    lane = lax.broadcasted_iota(jnp.int32, (1, QUERIES), 1)
    query_z = lax.broadcasted_iota(jnp.int32, (ZP, QUERIES), 1) % Z
    far_z = far_along(lax.broadcasted_iota(jnp.int32, (ZP, QUERIES), 0) - query_z)
    far_yz = [far_z + far_along(ky - lane // Z % CELLS) for ky in range(WIDE)]
    far_x = [far_along(kx - lane // (CELLS * Z)) for kx in rows_x]
    far = jnp.concatenate([yz + x for x in far_x for yz in far_yz], axis=0)
    return jnp.concatenate([far] * H, axis=1)


def forward(inputs, rows_x, w_kv, qbd, gabd, ks, vs, es, gps):
    kv = mm(inputs, w_kv).astype(BF16)
    ks[...] = kv[:, :C]
    vs[...] = kv[:, C:]
    scores = mm(kv[:, :C], qbd, NT)
    grad_probs = mm(kv[:, C:], gabd, NT)
    exps = jnp.exp(scores + outside(rows_x))
    es[...] = exps
    gps[...] = grad_probs
    weighted = jnp.sum(exps * grad_probs, axis=0, keepdims=True)
    return jnp.sum(exps, axis=0, keepdims=True), weighted


CENTRE = range(RADIUS, RADIUS + CELLS)
OUTER = [*range(RADIUS), *range(RADIUS + CELLS, WIDE)]


def rims_kernel(inputs, own, near, far):
    for x in range(CELLS):
        block = jnp.swapaxes(inputs[x].astype(F32), 0, 1)
        filled = jnp.concatenate([block, jnp.zeros((CELLS, ZP - ZE, C), F32)], axis=1)
        own[x] = filled.astype(BF16)
    odd = lax.axis_index("xl")
    near[...] = own[:, pl.ds(1 - odd, RADIUS)]
    far[...] = own[:, pl.ds(odd, RADIUS)]


def centre_kernel(own, ylo, yhi, cot, wqkv, wout, xs, qbd, gabd, ks, vs, es, gps, sums):
    xs[:, 0:RADIUS] = ylo[...]
    xs[:, RADIUS : RADIUS + CELLS] = own[...]
    xs[:, RADIUS + CELLS :] = yhi[...]
    inner = own[...].astype(F32)[:, :, RADIUS : RADIUS + Z, :].reshape(QUERIES, C).astype(BF16)
    cot2 = cot[...].astype(F32).reshape(QUERIES, C).astype(BF16)
    query = mm(inner, wqkv[:, :C]).astype(BF16).astype(F32) * HD ** (-0.5)
    grad_attn = mm(cot2, wout[...], NT).astype(BF16).astype(F32)
    head = lax.broadcasted_iota(jnp.int32, (QUERIES, C), 1) // HD
    for h in range(H):
        rows = slice(h * QUERIES, (h + 1) * QUERIES)
        qbd[rows, :] = jnp.where(head == h, query, 0.0).astype(BF16)
        gabd[rows, :] = jnp.where(head == h, grad_attn, 0.0).astype(BF16)
    exp_sum, weighted = forward(
        xs[...].reshape(-1, C), CENTRE, wqkv[:, C:], qbd[...], gabd[...], ks, vs, es, gps
    )
    sums[0:1, :] = exp_sum
    sums[1:2, :] = weighted


def main_kernel(
    own, cot, wqkv, xlo, xhi, xc, qbd, gabd, kc, vc, ec, gpc, sums,
    gkvc, gkvo, grad_query, dw,
    xo, ko, vo, eo, gpo, pbc, pbo, dsc, dso,
):
    xo[0:RADIUS] = xlo[...]
    xo[RADIUS:] = xhi[...]
    exp_sum, weighted = forward(
        xo[...].reshape(-1, C), OUTER, wqkv[:, C:], qbd[...], gabd[...], ko, vo, eo, gpo
    )
    inverse = 1.0 / (sums[0:1, :] + exp_sum)
    balance = (sums[1:2, :] + weighted) * inverse
    for es, gps, pbs, dss, gkvs in ((ec, gpc, pbc, dsc, gkvc), (eo, gpo, pbo, dso, gkvo)):
        probs = es[...] * inverse
        prob_bf = probs.astype(BF16)
        slopes = (probs * (gps[...] - balance)).astype(BF16)
        pbs[...] = prob_bf
        dss[...] = slopes
        gkvs[:, :C] = mm(slopes, qbd[...]).astype(BF16)
        gkvs[:, C:] = mm(prob_bf, gabd[...]).astype(BF16)

    def over_keys(parts):
        out = []
        for pair in range(H // 2):
            channels = slice(pair * 2 * HD, (pair + 1) * 2 * HD)
            lanes = slice(pair * 2 * QUERIES, (pair + 1) * 2 * QUERIES)
            full = sum(mm(values[:, channels], weights[:, lanes], TN) for values, weights in parts)
            out += [full[:HD, :QUERIES], full[HD:, QUERIES:]]
        return jnp.concatenate(out, axis=0)

    inner = own[...].astype(F32)[:, :, RADIUS : RADIUS + Z, :].reshape(QUERIES, C).astype(BF16)
    cot2 = cot[...].astype(F32).reshape(QUERIES, C).astype(BF16)
    attended = over_keys(((vc, pbc), (vo, pbo))).astype(BF16)
    grad_q = over_keys(((kc, dsc), (ko, dso))) * HD ** (-0.5)
    dw_kv = mm(xc[...].reshape(-1, C), gkvc[...], TN) + mm(xo[...].reshape(-1, C), gkvo[...], TN)
    grad_q = grad_q.T.astype(BF16)
    grad_query[...] = grad_q
    dw_out = mm(attended, cot2).astype(BF16)
    dw_q = mm(inner, grad_q, TN).astype(BF16)
    slot = 0
    for part in (dw_q, dw_kv.astype(BF16), dw_out):
        for start in range(0, part.shape[1], 128):
            for half in range(2):
                dw[half, slot] = part[half * 128 : (half + 1) * 128, start : start + 128]
            slot += 1


def inputs_kernel(gkvc, gkvo, grad_query, wqkv, grad_lo, grad_mid, grad_hi):
    outer = mm(gkvo[...], wqkv[:, C:], NT).astype(BF16).reshape(2 * RADIUS, WIDE, ZP, C)
    grad_lo[...] = outer[:RADIUS]
    grad_hi[...] = outer[RADIUS:]
    grad_mid[...] = mm(gkvc[...], wqkv[:, C:], NT).reshape(CELLS, WIDE, ZP, C)
    from_query = mm(grad_query[...], wqkv[:, :C], NT).reshape(CELLS, CELLS, Z, C)
    grad_mid[:, RADIUS : RADIUS + CELLS, RADIUS : RADIUS + Z, :] += from_query


def kernel_call(kernel, outs, args, scratch=(), flops=0, mib=24):
    whole = pl.BlockSpec(memory_space=pltpu.VMEM)
    return pl.pallas_call(
        kernel,
        out_shape=tuple(jax.ShapeDtypeStruct(shape, kind) for shape, kind in outs),
        in_specs=[whole] * len(args),
        out_specs=(whole,) * len(outs),
        scratch_shapes=[pltpu.VMEM(shape, kind) for shape, kind in scratch],
        cost_estimate=pl.CostEstimate(flops=flops, bytes_accessed=4 * 2**20, transcendentals=0),
        compiler_params=pltpu.CompilerParams(vmem_limit_bytes=mib * 2**20),
    )(*args)


NC_ = CELLS * ROWS
NO_ = 2 * RADIUS * ROWS


def centre(own, ylo, yhi, cot, wqkv, wout):
    outs = (
        ((CELLS, WIDE, ZP, C), BF16),
        ((LANES, C), BF16),
        ((LANES, C), BF16),
        ((NC_, C), BF16),
        ((NC_, C), BF16),
        ((NC_, LANES), F32),
        ((NC_, LANES), F32),
        ((2, LANES), F32),
    )
    return kernel_call(centre_kernel, outs, (own, ylo, yhi, cot, wqkv, wout), flops=10**9)


def main(own, cot, wqkv, xlo, xhi, held):
    outs = (
        ((NC_, 2 * C), BF16),
        ((NO_, 2 * C), BF16),
        ((QUERIES, C), BF16),
        ((2, 8, 128, 128), BF16),
    )
    scratch = (
        ((2 * RADIUS, WIDE, ZP, C), BF16),
        ((NO_, C), BF16),
        ((NO_, C), BF16),
        ((NO_, LANES), F32),
        ((NO_, LANES), F32),
        ((NC_, LANES), BF16),
        ((NO_, LANES), BF16),
        ((NC_, LANES), BF16),
        ((NO_, LANES), BF16),
    )
    args = (own, cot, wqkv, xlo, xhi, *held)
    return kernel_call(main_kernel, outs, args, scratch, flops=3 * 10**9)


def through_inputs(gkvc, gkvo, grad_query, wqkv):
    outs = (
        ((RADIUS, WIDE, ZP, C), BF16),
        ((CELLS, WIDE, ZP, C), F32),
        ((RADIUS, WIDE, ZP, C), BF16),
    )
    return kernel_call(inputs_kernel, outs, (gkvc, gkvo, grad_query, wqkv), flops=10**9)


def own_rims(inputs):
    rim = ((CELLS, RADIUS, ZP, C), BF16)
    outs = (((CELLS, CELLS, ZP, C), BF16), rim, rim)
    return kernel_call(rims_kernel, outs, (inputs.transpose(0, 2, 1, 3),), mib=4)


def local_grads(own, ylo, yhi, xlo, xhi, cot, wqkv, wout):
    held = centre(own, ylo, yhi, cot, wqkv, wout)
    gkvc, gkvo, grad_query, dw = main(own, cot, wqkv, xlo, xhi, held)
    return (*through_inputs(gkvc, gkvo, grad_query, wqkv), dw)


def to_near(block, axes):
    return lax.ppermute(block, axes, [(i, i ^ 1) for i in range(lax.axis_size(axes))])


def to_far(block, axes):
    size = lax.axis_size(axes)
    pairs = [(i, (i + 1 if i % 2 else i - 1) % size) for i in range(size)]
    return lax.ppermute(block, axes, pairs)


def neighbours(easy, hard, axes):
    from_far = to_far(hard, axes)
    return to_near(easy, axes), from_far


def exchanged(low, high, axes):
    first = lax.axis_index(axes) % 2 == 0
    near, far = neighbours(jnp.where(first, high, low), jnp.where(first, low, high), axes)
    return jnp.where(first, far, near), jnp.where(first, near, far)


def rims(block, dim, axes):
    odd = lax.axis_index(axes) % 2
    easy = lax.dynamic_slice_in_dim(block, 1 - odd, RADIUS, dim)
    hard = lax.dynamic_slice_in_dim(block, odd, RADIUS, dim)
    near, far = neighbours(easy, hard, axes)
    return jnp.where(odd == 0, far, near), jnp.where(odd == 0, near, far)


def last_kernel(half, other, middle, before, after, wqkv, wout, grads):
    core = lax.axis_index("core")
    for part, place in ((half, core), (other, 1 - core)):
        rows = pl.ds(pl.multiple_of(place * 128, 128), 128)
        for slot in range(8):
            tile = part[slot].astype(F32)
            if slot < 6:
                wqkv[rows, slot * 128 : (slot + 1) * 128] = tile
            else:
                wout[rows, (slot - 6) * 128 : (slot - 5) * 128] = tile
    columns = []
    for y in range(CELLS):
        column = middle[:, y]
        if y < RADIUS:
            column += before[:, y].astype(F32)
        if y >= CELLS - RADIUS:
            column += after[:, y - CELLS + RADIUS].astype(F32)
        columns.append(column[:, :ZE])
    grads[...] = jnp.stack(columns, axis=2).astype(BF16)


def last(half, other, middle, before, after):
    whole = pl.BlockSpec(memory_space=pltpu.VMEM)
    wqkv, wout, grads = pl.pallas_call(
        last_kernel,
        out_shape=(
            jax.ShapeDtypeStruct((C, 3 * C), F32),
            jax.ShapeDtypeStruct((C, C), F32),
            jax.ShapeDtypeStruct((CELLS, ZE, CELLS, C), BF16),
        ),
        in_specs=[whole] * 5,
        out_specs=(whole,) * 3,
        compiler_params=pltpu.CompilerParams(vmem_limit_bytes=10 * 2**20),
    )(half.reshape(8, 128, 128), other.reshape(8, 128, 128), middle, before, after)
    return grads.transpose(0, 2, 1, 3), wqkv, wout


GX = ("xh", "y", "core")
GY = ("z", "xl")
PLANE = ("xl", "y", "xh")


def summed_weights(dw):
    core = lax.axis_index("core")
    halves = dw.reshape(2, 16, 64, 128)
    mine = lax.dynamic_index_in_dim(halves, core, 0, keepdims=False)
    other = lax.dynamic_index_in_dim(halves, 1 - core, 0, keepdims=False)
    swap = [(0, 1), (1, 0)]
    half = (mine.astype(F32) + lax.ppermute(other, "core", swap).astype(F32)).astype(BF16)
    chunks = lax.all_to_all(half, PLANE, 0, 0)
    chunk = jnp.sum(chunks.astype(F32), axis=0).astype(BF16)
    columns = lax.all_to_all(jnp.broadcast_to(chunk[None], (8, 64, 128)), "z", 0, 0)
    chunk = jnp.sum(columns.astype(F32), axis=0).astype(BF16)
    half = lax.all_to_all(jnp.broadcast_to(chunk[None], (16, 64, 128)), PLANE, 0, 0)
    other = lax.ppermute(half, "core", swap)
    return half, other


def body(inputs, cotangent, w_qkv, w_out):
    own, near, far = own_rims(inputs)
    far, near = to_far(far, GY), to_near(near, GY)
    first = lax.axis_index(GY) % 2 == 0
    ylo, yhi = jnp.where(first, far, near), jnp.where(first, near, far)
    wide = jnp.concatenate([ylo, own, yhi], axis=1)
    xlo, xhi = rims(wide, 0, GX)
    grad_lo, grad_mid, grad_hi, dw = local_grads(
        own, ylo, yhi, xlo, xhi, cotangent, w_qkv, w_out
    )
    from_before, from_next = exchanged(grad_lo, grad_hi, GX)
    from_before, from_next = from_before.astype(F32), from_next.astype(F32)
    rest = ((0, 0), (0, 0), (0, 0))
    grad_mid = (
        grad_mid
        + jnp.pad(from_next, ((CELLS - RADIUS, 0),) + rest)
        + jnp.pad(from_before, ((0, CELLS - RADIUS),) + rest)
    )
    middle = grad_mid[:, RADIUS : RADIUS + CELLS]
    low = grad_mid[:, :RADIUS].astype(BF16)
    high = grad_mid[:, RADIUS + CELLS :].astype(BF16)
    from_before, from_next = exchanged(low, high, GY)
    half, other = summed_weights(dw)
    return last(half, other, middle, from_before, from_next)


def solution(mesh):
    fine = Mesh(mesh.devices.reshape(2, 4, 2, 8, 2), ("xh", "y", "core", "z", "xl"))
    split = P(GX, GY, None, None)
    return jax.shard_map(
        body,
        mesh=fine,
        in_specs=(split, split, P(), P()),
        out_specs=(split, P(), P()),
        check_vma=False,
    )
```
